32 devices in a mesh: row: 16 (over z, y, core), col: 2 (over x).
Axes of the slice: x: 2, y: 2, z: 4, core: 2. Of those that a mesh axis runs over, the one named last changes fastest.
Arguments:
- colloc: bfloat16 [2, 1024, 9216], P(None, 'row'), may hold values from -6 to 6
- coefficients: bfloat16 [2, 9216, 512], P(None, 'row'), may hold values from -0.0625 to 0.0625
- occupied: int32 [2], replicated, may hold values from 256 to 512
- offsets: int32 [2, 2], replicated, may hold values from 0 to 1024
Outputs:
- exchange_matrix: bfloat16 [9216, 2, 9216], P('col', None, 'row')
The draws below stay inside these ranges and needn't reach their ends.
Inputs may be any that keep to these rules, and one draw needn't show every extreme that they name: occupied[s] is the number of occupied orbitals of spin s. offsets[s, k] is the first point of panel k of spin s on the line of 73728 points; both panels lie within the first 1536 points and may intersect.
All inputs are finite; a program needn't handle non-finite values.
Results may differ from the reference program's by a relative error of at most 0.019.
Values may be sent and summed in bfloat16 or wider, within the bound.
A program may use at most 128 MiB of HBM per device.

```python
import math
import jax
import jax.numpy as jnp
from jax import lax

NB = 9216
OCC = 512
SPINS = 2
PR = 64
PTS = 1024
PANEL = 512
SCREEN = 64
N_ROW = 16
N_COL = 2


def place_ends(entries, own_key, low, largest):
    index_at = [jax.random.randint(jax.random.fold_in(own_key, axis), (), 0, length) for axis, length in enumerate(entries.shape)]
    main_axis = entries.shape.index(max(entries.shape))
    neighbour = index_at[:main_axis] + [(index_at[main_axis] + 1) % entries.shape[main_axis]] + index_at[main_axis + 1:]
    return entries.at[tuple(index_at)].set(low).at[tuple(neighbour)].set(largest)


def level_of(key, extent, cuts, least, top_value):
    def one(axis_at, blocks):
        heights = jax.random.uniform(jax.random.fold_in(jax.random.fold_in(key, 6), axis_at), (blocks,), jnp.float32, least / len(cuts), top_value / len(cuts))
        return jnp.repeat(jnp.exp(heights), extent[axis_at] // blocks).reshape((-1,) + (1,) * (len(extent) - axis_at - 1))

    gain = one(*cuts[0])
    for cut in cuts[1:]:
        gain = gain * one(*cut)
    return gain


def gaussian(stream_key, dims, scale, reach, pieces=(), held_as=jnp.bfloat16):
    values = scale * jax.random.normal(stream_key, dims, jnp.float32)
    if pieces:
        values = values * level_of(stream_key, dims, pieces, -0.22, 0.18)
    return jnp.clip(values, -reach, reach).astype(held_as)


def setup_inputs(seed: int = 0) -> dict:
    splits = jax.random.split(jax.random.key(seed), 5)
    return {
        "colloc": gaussian(splits[0], (SPINS, PTS, NB), 1.0, 6.0, ((1, 16),)),
        "coefficients": gaussian(splits[1], (SPINS, NB, OCC), NB ** -0.5, 0.0625, ((1, 16),)),
        "occupied": jax.random.randint(splits[2], (SPINS,), OCC // 2, OCC + 1).astype(jnp.int32),
        "offsets": place_ends(jax.random.randint(splits[3], (SPINS, 2), 0, 2 * PANEL + 1), jax.random.fold_in(splits[3], 1), 0, 2 * PANEL).astype(jnp.int32),
    }


def point_positions(point_ids, offsets, panel_len):
    first = jnp.where(point_ids[None, :] // panel_len == 0, offsets[:, 0:1], offsets[:, 1:2])
    return (first + point_ids[None, :] % panel_len).astype(jnp.float32)

def reference(colloc, coefficients, occupied, offsets):
    orbitals = jnp.einsum('spm,smi->spi', colloc.astype(jnp.float32), coefficients.astype(jnp.float32))
    occupied_mask = jnp.arange(OCC, dtype=jnp.int32)[None, :] < occupied[:, None]
    orbitals = jnp.where(occupied_mask[:, None, :], orbitals, 0.0).astype(jnp.bfloat16)
    point_ids = jnp.arange(PTS, dtype=jnp.int32)
    positions = point_positions(point_ids, offsets, PANEL)
    kernel = 1.0 / (1.0 + jnp.abs(positions[:, :, None] - positions[:, None, :]) / SCREEN)
    density = jnp.einsum('spi,sqi->spq', orbitals.astype(jnp.float32), orbitals.astype(jnp.float32))
    mixed_kernel = (kernel * density / OCC).astype(jnp.bfloat16)
    weighted = jnp.einsum('spq,sqn->spn', mixed_kernel.astype(jnp.float32), colloc.astype(jnp.float32)).astype(jnp.bfloat16)
    norm_factor = 1.0 / math.sqrt(PTS)
    sub_rows = PR // N_COL
    left_split = colloc.reshape(SPINS, N_ROW, N_COL, sub_rows, NB)
    right_split = weighted.reshape(SPINS, N_ROW, N_COL, sub_rows, NB)
    result = jnp.zeros((NB, SPINS, NB), jnp.float32)
    for group in range(N_COL):
        left_rows = left_split[:, :, group].astype(jnp.float32)
        right_rows = right_split[:, :, group].astype(jnp.float32)
        group_term = jnp.einsum('sxkm,sxkn->msn', left_rows, right_rows) * norm_factor
        rounded = lax.optimization_barrier(group_term.astype(jnp.bfloat16))
        result = result + rounded.astype(jnp.float32)
    return result.astype(jnp.bfloat16)
```

```python
import math

import jax
import jax.numpy as jnp
from jax import lax
from jax.sharding import PartitionSpec as P


def positions_of(offsets, points, panel_len):
    ids = jnp.arange(points, dtype=jnp.int32)
    first = jnp.where(ids[None, :] // panel_len == 0, offsets[:, 0:1], offsets[:, 1:2])
    return (first + ids[None, :] % panel_len).astype(jnp.float32)


def local(colloc, coefficients, occupied, offsets):
    rows = lax.axis_size("row")
    cols = lax.axis_size("col")
    row = lax.axis_index("row")
    col = lax.axis_index("col")
    spins, own_points, basis = colloc.shape
    depth, slots = coefficients.shape[1:]
    points = own_points * rows
    panel_len = points // 2
    screen_len = panel_len // 8
    share = basis // cols
    part = depth // cols
    own_coefficients = lax.dynamic_slice_in_dim(coefficients, col * part, part, 1)
    coefficient_share = lax.all_gather(own_coefficients, "row", axis=1, tiled=True)
    own_share = lax.dynamic_slice_in_dim(colloc, col * share, share, 2)
    basis_share = lax.all_gather(own_share, "row", axis=1, tiled=True)
    cut = colloc.reshape(spins, own_points, rows, cols, part)
    cut = lax.dynamic_index_in_dim(cut, col, 3, keepdims=False).reshape(spins, own_points, rows * part)
    partial_value = jnp.einsum("spm,smi->spi", cut, coefficient_share, preferred_element_type=jnp.float32)
    summed = lax.psum(partial_value, "col")
    occupied_mask = jnp.arange(slots, dtype=jnp.int32)[None, :] < occupied[:, None]
    own_orbitals = jnp.where(occupied_mask[:, None, :], summed, 0.0).astype(jnp.bfloat16)
    orbitals = lax.all_gather(own_orbitals, "row", axis=1, tiled=True)
    place = positions_of(offsets, points, panel_len)
    kernel = 1.0 / (1.0 + jnp.abs(place[:, :, None] - place[:, None, :]) / screen_len)
    density = jnp.einsum("spi,sqi->spq", orbitals, orbitals, preferred_element_type=jnp.float32)
    mixed_kernel = (kernel * density / slots).astype(jnp.bfloat16)
    per_col = rows // cols
    own_window = lax.dynamic_slice_in_dim(basis_share, row % per_col * depth, depth, 2)
    window = lax.psum(jnp.where(row // per_col == col, own_window, jnp.bfloat16(0)), "col")
    weighted = jnp.einsum("spq,sqn->spn", mixed_kernel, window, preferred_element_type=jnp.float32)
    weighted = weighted.astype(jnp.bfloat16)
    result = jnp.einsum("spm,spn->msn", basis_share, weighted, preferred_element_type=jnp.float32)
    return (result * (1.0 / math.sqrt(points))).astype(jnp.bfloat16)


def solution(mesh):
    placed = (P(None, "row", None), P(None, "row", None), P(), P())
    return jax.shard_map(
        local, mesh=mesh, in_specs=placed, out_specs=P("col", None, "row"), check_vma=False
    )
```

```python
import functools
import math

import jax
import jax.numpy as jnp
from jax import lax
from jax.experimental import pallas as pl
from jax.experimental.pallas import tpu as pltpu
from jax.sharding import PartitionSpec as P

MESH = pl.DeviceIdType.MESH
LANES = 128


def positions_of(offsets, points, panel_len):
    ids = jnp.arange(points, dtype=jnp.int32)
    first = jnp.where(ids[None, :] // panel_len == 0, offsets[:, 0:1], offsets[:, 1:2])
    return (first + ids[None, :] % panel_len).astype(jnp.float32)


def window_lanes(depth):
    over = LANES - math.gcd(depth, LANES)
    return -(-(depth + over) // LANES) * LANES


class Ring:
    def __init__(self, place, own, piece, ring_send, ring_recv, pair_send, pair_recv):
        self.place, self.own, self.piece = place, own, piece
        self.ring_send, self.ring_recv = ring_send, ring_recv
        self.pair_send, self.pair_recv = pair_send, pair_recv

    def origin(self, way, step, core):
        chips = self.place["chips"]
        back = -step if way == 0 else step
        return self.place["chip_at"](lax.rem(self.place["position"] + back + chips, chips)) * 2 + core

    def source(self, way, step):
        return self.own(way) if step == 0 else self.piece(way, self.origin(way, step, self.place["core"]))

    def hop(self, way, step):
        target = self.place["next"] if way == 0 else self.place["previous"]
        return pltpu.make_async_remote_copy(
            src_ref=self.source(way, step),
            dst_ref=self.piece(way, self.origin(way, step, self.place["core"])),
            send_sem=self.ring_send.at[way, step % 2],
            recv_sem=self.ring_recv.at[way, step],
            device_id=(target, self.place["col"]),
            device_id_type=MESH,
        )

    def landed(self, way, step):
        return pltpu.make_async_remote_copy(
            src_ref=self.source(way, step),
            dst_ref=self.piece(way, self.origin(way, step + 1, self.place["core"])),
            send_sem=self.ring_send.at[way, step % 2],
            recv_sem=self.ring_recv.at[way, step],
            device_id=(self.place["next"], self.place["col"]),
            device_id_type=MESH,
        )

    def hand(self, way, step):
        return pltpu.make_async_remote_copy(
            src_ref=self.source(way, step),
            dst_ref=self.piece(way, self.origin(way, step, self.place["core"])),
            send_sem=self.pair_send.at[way, step % 2],
            recv_sem=self.pair_recv.at[way, step],
            device_id=(self.place["sibling"], self.place["col"]),
            device_id_type=MESH,
        )

    def handed(self, way, step):
        return pltpu.make_async_remote_copy(
            src_ref=self.source(way, step),
            dst_ref=self.piece(way, self.origin(way, step, 1 - self.place["core"])),
            send_sem=self.pair_send.at[way, step % 2],
            recv_sem=self.pair_recv.at[way, step],
            device_id=(self.place["sibling"], self.place["col"]),
            device_id_type=MESH,
        )

    def begin(self):
        for way in (0, 1):
            self.hop(way, 0).start()
        for way in (0, 1):
            self.hand(way, 0).start()

    def advance(self, step):
        chips = self.place["chips"]
        for way in (0, 1):
            self.landed(way, step).wait_recv()
            if step + 1 < chips - 1:
                if step >= 1:
                    self.hop(way, step - 1).wait_send()
                self.hop(way, step + 1).start()
            if step >= 1:
                self.hand(way, step - 1).wait_send()
            self.hand(way, step + 1).start()

    def finish_sends(self):
        chips = self.place["chips"]
        for way in (0, 1):
            for step in range(max(chips - 3, 0), chips - 1):
                self.hop(way, step).wait_send()
            for step in range(chips - 2, chips):
                self.hand(way, step).wait_send()


def transfers(
    rows, cols, slot_blocks, colloc, coefficients, basis_share, window, orbitals,
    all_coefficients, own_colloc, own_orbitals, total, local_sem,
    c_rs, c_rr, c_ps, c_pr, b_rs, b_rr, b_ps, b_pr, o_rs, o_rr, o_ps, o_pr,
    x_send, x_recv, w_local, y_send, y_recv,
):
    row, col = lax.axis_index("row"), lax.axis_index("col")
    spins, own_points, basis = colloc.shape
    depth, slots = coefficients.shape[1:]
    share = basis // cols
    width = window.shape[2]
    per_col = rows // cols
    chips = rows // 2
    side = chips // 2
    core, chip = row % 2, row // 2

    def chip_at(position):
        high = position // side
        return (position + high * (chips - 1 - 2 * position)) * 2 + high

    position = chip // 2 + (chip % 2) * (chips - 1 - 2 * (chip // 2))
    place = dict(
        chips=chips, chip_at=chip_at, position=position, core=core, col=col,
        next=chip_at(lax.rem(position + 1, chips)) * 2 + core,
        previous=chip_at(lax.rem(position + chips - 1, chips)) * 2 + core,
        sibling=chip * 2 + 1 - core,
    )
    other_cols = [lax.rem(col + shift, cols) for shift in range(1, cols)]
    spin, block = col % spins, col // spins
    block_len = slots // slot_blocks
    block_lanes = pl.ds(pl.multiple_of(block * block_len, LANES), block_len)
    share_start = pl.multiple_of(col * share, LANES)
    half = depth // 2

    barrier = pltpu.get_barrier_semaphore()
    for other in (place["next"], place["previous"], place["sibling"]):
        pl.semaphore_signal(barrier, inc=1, device_id=(other, col), device_id_type=MESH)
    for other in other_cols:
        pl.semaphore_signal(barrier, inc=1, device_id=(row, other), device_id_type=MESH)
    pl.semaphore_wait(barrier, 3 + len(other_cols))

    def point_rows(at):
        return pl.ds(pl.multiple_of(at * own_points, own_points), own_points)

    coefficient_ring = Ring(
        place,
        lambda way: coefficients.at[spin, pl.ds(way * half, half), block_lanes],
        lambda way, at: all_coefficients.at[pl.ds(pl.multiple_of(at * depth + way * half, 16), half), :],
        c_rs, c_rr, c_ps, c_pr,
    )
    basis_ring = Ring(
        place,
        lambda way: colloc.at[way, :, pl.ds(share_start, share)],
        lambda way, at: basis_share.at[way, point_rows(at), :],
        b_rs, b_rr, b_ps, b_pr,
    )
    orbital_ring = Ring(
        place,
        lambda way: own_orbitals.at[way],
        lambda way, at: orbitals.at[way, point_rows(at), :],
        o_rs, o_rr, o_ps, o_pr,
    )

    coefficient_ring.begin()
    basis_ring.begin()
    local = [
        pltpu.make_async_copy(
            coefficients.at[spin, :, block_lanes],
            all_coefficients.at[pl.ds(pl.multiple_of(row * depth, 16), depth), :],
            local_sem.at[0],
        ),
        pltpu.make_async_copy(colloc.at[spin], own_colloc, local_sem.at[1]),
        pltpu.make_async_copy(
            colloc.at[:, :, pl.ds(share_start, share)],
            basis_share.at[:, point_rows(row), :],
            local_sem.at[2],
        ),
    ]
    for copy in local:
        copy.start()

    owner = row // per_col == col
    first_lane = pl.multiple_of((row % per_col) * depth // LANES * LANES, LANES)

    def window_piece(way, step, at_core):
        at = basis_ring.origin(way, step, at_core)
        relation = at_core_index(at_core)
        source = basis_share.at[way, point_rows(at), pl.ds(first_lane, width)]
        target = window.at[way, point_rows(at), :]
        here = pltpu.make_async_copy(source, target, w_local.at[relation, way, step % 2])
        away = [
            pltpu.make_async_remote_copy(
                src_ref=source, dst_ref=target,
                send_sem=x_send.at[n, relation, way, step % 2],
                recv_sem=x_recv.at[relation, way, step],
                device_id=(row, other), device_id_type=MESH,
            )
            for n, other in enumerate(other_cols)
        ]
        return here, away

    def at_core_index(at_core):
        return 0 if at_core is core else 1

    other_core = 1 - core

    def start_window(step, at_core):
        @pl.when(owner)
        def _():
            for way in (0, 1):
                if step >= 2:
                    here, away = window_piece(way, step - 2, at_core)
                    here.wait()
                    for copy in away:
                        copy.wait_send()
                here, away = window_piece(way, step, at_core)
                for copy in away:
                    copy.start()
                here.start()

    def wait_handed(ring, step):
        for way in (0, 1):
            ring.handed(way, step).wait_recv()

    def basis_step(step):
        basis_ring.advance(step)
        if step == 0:
            local[2].wait()
            start_window(0, core)
        start_window(step + 1, core)
        wait_handed(basis_ring, step)
        start_window(step, other_core)

    last = chips - 1
    done = 0
    early = max(last * 2 // 7, 1)
    for step in range(last):
        coefficient_ring.advance(step)
        if (step + 1) * early // last > done:
            basis_step(done)
            done += 1
    for step in range(chips):
        wait_handed(coefficient_ring, step)
    local[0].wait()
    local[1].wait()

    total[...] = jnp.zeros_like(total)
    chunk = 9 * LANES if basis % (9 * LANES) == 0 else LANES

    @pl.loop(0, basis // chunk)
    def _(i):
        at = pl.ds(pl.multiple_of(i * chunk, chunk), chunk)
        total[...] += jnp.dot(own_colloc[:, at], all_coefficients[at, :], preferred_element_type=jnp.float32)

    own_orbitals[spin, :, block_lanes] = total[...].astype(jnp.bfloat16)
    swaps = [
        pltpu.make_async_remote_copy(
            src_ref=own_orbitals.at[spin, :, block_lanes],
            dst_ref=own_orbitals.at[spin, :, block_lanes],
            send_sem=y_send.at[n], recv_sem=y_recv.at[n],
            device_id=(row, other), device_id_type=MESH,
        )
        for n, other in enumerate(other_cols)
    ]
    for copy in swaps:
        copy.start()
    for n in range(cols - 1):
        came = lax.rem(col + cols - 1 - n, cols)
        lanes = pl.ds(pl.multiple_of(came // spins * block_len, LANES), block_len)
        pltpu.make_async_remote_copy(
            src_ref=own_orbitals.at[spin, :, block_lanes],
            dst_ref=own_orbitals.at[came % spins, :, lanes],
            send_sem=y_send.at[n], recv_sem=y_recv.at[n],
            device_id=(row, came), device_id_type=MESH,
        ).wait_recv()
    orbital_ring.begin()
    own_out = pltpu.make_async_copy(own_orbitals, orbitals.at[:, point_rows(row), :], local_sem.at[3])
    own_out.start()
    left, sent = last - done, 0
    for n in range(left):
        basis_step(done)
        done += 1
        while sent < last and sent < -(-(n + 1) * last // max(left - 1, 1)):
            orbital_ring.advance(sent)
            sent += 1
    wait_handed(basis_ring, last)
    start_window(last, other_core)
    for step in range(chips):
        wait_handed(orbital_ring, step)
    own_out.wait()
    for copy in swaps:
        copy.wait_send()
    for ring in (coefficient_ring, basis_ring, orbital_ring):
        ring.finish_sends()

    @pl.when(owner)
    def _():
        for at_core in (core, other_core):
            for step in (last - 1, last):
                for way in (0, 1):
                    here, away = window_piece(way, step, at_core)
                    here.wait()
                    for copy in away:
                        copy.wait_send()

    @pl.when(jnp.logical_not(owner))
    def _():
        for at_core in (core, other_core):
            for step in range(chips):
                for way in (0, 1):
                    window_piece(way, step, at_core)[1][0].wait_recv()


def gathered(colloc, coefficients, rows, cols):
    spins, own_points, basis = colloc.shape
    depth, slots = coefficients.shape[1:]
    points, share, chips = own_points * rows, basis // cols, rows // 2
    slot_blocks = cols // spins
    block_len = slots // slot_blocks
    dma = pltpu.SemaphoreType.DMA
    ring = [dma((2, 2)), dma((2, chips - 1)), dma((2, 2)), dma((2, chips))]
    anywhere = pl.BlockSpec(memory_space=pl.ANY)
    return pl.pallas_call(
        functools.partial(transfers, rows, cols, slot_blocks),
        out_shape=(
            jax.ShapeDtypeStruct((spins, points, share), colloc.dtype),
            jax.ShapeDtypeStruct((spins, points, window_lanes(depth)), colloc.dtype),
            jax.ShapeDtypeStruct((spins, points, slots), colloc.dtype),
        ),
        in_specs=[anywhere] * 2,
        out_specs=(anywhere,) * 3,
        scratch_shapes=[
            pltpu.VMEM((basis, block_len), colloc.dtype),
            pltpu.VMEM((own_points, basis), colloc.dtype),
            pltpu.VMEM((spins, own_points, slots), colloc.dtype),
            pltpu.VMEM((own_points, block_len), jnp.float32),
            dma((4,)),
            *ring, *ring, *ring,
            dma((cols - 1, 2, 2, 2)), dma((2, 2, chips)), dma((2, 2, 2)),
            dma((cols - 1,)), dma((cols - 1,)),
        ],
        compiler_params=pltpu.CompilerParams(
            collective_id=0, has_side_effects=True, vmem_limit_bytes=24 * 2**20
        ),
    )(colloc, coefficients)


def local(colloc, coefficients, occupied, offsets):
    rows = lax.axis_size("row")
    cols = lax.axis_size("col")
    row = lax.axis_index("row")
    spins, own_points, basis = colloc.shape
    depth, slots = coefficients.shape[1:]
    points = own_points * rows
    panel_len = points // 2
    screen_len = panel_len // 8
    basis_share, window, orbitals = gathered(colloc, coefficients, rows, cols)
    occupied_mask = jnp.arange(slots, dtype=jnp.int32)[None, :] < occupied[:, None]
    orbitals = jnp.where(occupied_mask[:, None, :], orbitals, jnp.bfloat16(0))
    place = positions_of(offsets, points, panel_len)
    kernel = 1.0 / (1.0 + jnp.abs(place[:, :, None] - place[:, None, :]) / screen_len)
    density = jnp.einsum("spi,sqi->spq", orbitals, orbitals, preferred_element_type=jnp.float32)
    mixed_kernel = (kernel * density / slots).astype(jnp.bfloat16)
    weighted = jnp.einsum("spq,sqn->spn", mixed_kernel, window, preferred_element_type=jnp.float32)
    weighted = lax.dynamic_slice_in_dim(weighted.astype(jnp.bfloat16), row * depth % LANES, depth, 2)
    result = jnp.einsum("spm,spn->msn", basis_share, weighted, preferred_element_type=jnp.float32)
    return (result * (1.0 / math.sqrt(points))).astype(jnp.bfloat16)


def solution(mesh):
    placed = (P(None, "row", None), P(None, "row", None), P(), P())
    return jax.shard_map(
        local, mesh=mesh, in_specs=placed, out_specs=P("col", None, "row"), check_vma=False
    )
```

```python
import functools
import math

import jax
import jax.numpy as jnp
from jax import lax
from jax.experimental import pallas as pl
from jax.experimental.pallas import tpu as pltpu
from jax.sharding import PartitionSpec as P

MESH = pl.DeviceIdType.MESH
LANES = 128


def window_lanes(depth):
    over = LANES - math.gcd(depth, LANES)
    return -(-(depth + over) // LANES) * LANES


class Ring:
    def __init__(self, chains, place, own, piece, ring_send, ring_recv, pair_send, pair_recv):
        self.ways = range(2 * chains)
        self.place, self.own, self.piece = place, own, piece
        self.ring_send, self.ring_recv = ring_send, ring_recv
        self.pair_send, self.pair_recv = pair_send, pair_recv

    def origin(self, way, step, core):
        chips = self.place["chips"]
        back = -step if way % 2 == 0 else step
        return self.place["chip_at"](lax.rem(self.place["position"] + back + chips, chips)) * 2 + core

    def source(self, way, step):
        return self.own(way) if step == 0 else self.piece(way, self.origin(way, step, self.place["core"]))

    def hop(self, way, step):
        target = self.place["next"] if way % 2 == 0 else self.place["previous"]
        return pltpu.make_async_remote_copy(
            src_ref=self.source(way, step),
            dst_ref=self.piece(way, self.origin(way, step, self.place["core"])),
            send_sem=self.ring_send.at[way, step % 2],
            recv_sem=self.ring_recv.at[way, step],
            device_id=(target, self.place["col"]),
            device_id_type=MESH,
        )

    def landed(self, way, step):
        return pltpu.make_async_remote_copy(
            src_ref=self.source(way, step),
            dst_ref=self.piece(way, self.origin(way, step + 1, self.place["core"])),
            send_sem=self.ring_send.at[way, step % 2],
            recv_sem=self.ring_recv.at[way, step],
            device_id=(self.place["next"], self.place["col"]),
            device_id_type=MESH,
        )

    def hand(self, way, step):
        return pltpu.make_async_remote_copy(
            src_ref=self.source(way, step),
            dst_ref=self.piece(way, self.origin(way, step, self.place["core"])),
            send_sem=self.pair_send.at[way, step % 2],
            recv_sem=self.pair_recv.at[way, step],
            device_id=(self.place["sibling"], self.place["col"]),
            device_id_type=MESH,
        )

    def handed(self, way, step):
        return pltpu.make_async_remote_copy(
            src_ref=self.source(way, step),
            dst_ref=self.piece(way, self.origin(way, step, 1 - self.place["core"])),
            send_sem=self.pair_send.at[way, step % 2],
            recv_sem=self.pair_recv.at[way, step],
            device_id=(self.place["sibling"], self.place["col"]),
            device_id_type=MESH,
        )

    def begin(self):
        for way in self.ways:
            self.hop(way, 0).start()
        for way in self.ways:
            self.hand(way, 0).start()

    def advance(self, step, chain=0):
        chips = self.place["chips"]
        for way in (2 * chain, 2 * chain + 1):
            self.landed(way, step).wait_recv()
            if step + 1 < chips - 1:
                if step >= 1:
                    self.hop(way, step - 1).wait_send()
                self.hop(way, step + 1).start()
            if step >= 1:
                self.hand(way, step - 1).wait_send()
            self.hand(way, step + 1).start()

    def finish_sends(self):
        chips = self.place["chips"]
        for way in self.ways:
            for step in range(max(chips - 3, 0), chips - 1):
                self.hop(way, step).wait_send()
            for step in range(chips - 2, chips):
                self.hand(way, step).wait_send()


def transfers(
    rows, cols, slot_blocks, occupied, offsets, colloc, coefficients, basis_share, window, mixed_out,
    orbitals, mixed, all_coefficients, own_colloc, own_orbitals, total, local_sem,
    c_rs, c_rr, c_ps, c_pr, b_rs, b_rr, b_ps, b_pr, o_rs, o_rr, o_ps, o_pr,
    x_send, x_recv, w_local, y_send, y_recv,
):
    row, col = lax.axis_index("row"), lax.axis_index("col")
    spins, own_points, basis = colloc.shape
    depth, slots = coefficients.shape[1:]
    share = basis // cols
    width = window.shape[2]
    per_col = rows // cols
    chips = rows // 2
    side = chips // 2
    core, chip = row % 2, row // 2

    def chip_at(position):
        high = position // side
        return (position + high * (chips - 1 - 2 * position)) * 2 + high

    position = chip // 2 + (chip % 2) * (chips - 1 - 2 * (chip // 2))
    place = dict(
        chips=chips, chip_at=chip_at, position=position, core=core, col=col,
        next=chip_at(lax.rem(position + 1, chips)) * 2 + core,
        previous=chip_at(lax.rem(position + chips - 1, chips)) * 2 + core,
        sibling=chip * 2 + 1 - core,
    )
    other_cols = [lax.rem(col + shift, cols) for shift in range(1, cols)]
    spin, block = col % spins, col // spins
    block_len = slots // slot_blocks
    block_lanes = pl.ds(pl.multiple_of(block * block_len, LANES), block_len)
    share_start = pl.multiple_of(col * share, LANES)
    half = depth // 2

    barrier = pltpu.get_barrier_semaphore()
    for other in (place["next"], place["previous"], place["sibling"]):
        pl.semaphore_signal(barrier, inc=1, device_id=(other, col), device_id_type=MESH)
    for other in other_cols:
        pl.semaphore_signal(barrier, inc=1, device_id=(row, other), device_id_type=MESH)
    pl.semaphore_wait(barrier, 3 + len(other_cols))

    def point_rows(at):
        return pl.ds(pl.multiple_of(at * own_points, own_points), own_points)

    sub = own_points // 2

    def sub_rows(way, at):
        return pl.ds(pl.multiple_of(at * own_points + way // 2 * sub, sub), sub)

    coefficient_ring = Ring(
        1,
        place,
        lambda way: coefficients.at[spin, pl.ds(way * half, half), block_lanes],
        lambda way, at: all_coefficients.at[pl.ds(pl.multiple_of(at * depth + way * half, 16), half), :],
        c_rs, c_rr, c_ps, c_pr,
    )
    basis_ring = Ring(
        2,
        place,
        lambda way: colloc.at[way % 2, pl.ds(way // 2 * sub, sub), pl.ds(share_start, share)],
        lambda way, at: basis_share.at[way % 2, sub_rows(way, at), :],
        b_rs, b_rr, b_ps, b_pr,
    )
    orbital_ring = Ring(
        1,
        place,
        lambda way: own_orbitals.at[way],
        lambda way, at: orbitals.at[way, point_rows(at), :],
        o_rs, o_rr, o_ps, o_pr,
    )

    coefficient_ring.begin()
    basis_ring.begin()
    local = [
        pltpu.make_async_copy(
            coefficients.at[spin, :, block_lanes],
            all_coefficients.at[pl.ds(pl.multiple_of(row * depth, 16), depth), :],
            local_sem.at[0],
        ),
        pltpu.make_async_copy(colloc.at[spin], own_colloc, local_sem.at[1]),
        pltpu.make_async_copy(
            colloc.at[:, :, pl.ds(share_start, share)],
            basis_share.at[:, point_rows(row), :],
            local_sem.at[2],
        ),
    ]
    for copy in local:
        copy.start()

    owner = row // per_col == col
    first_lane = pl.multiple_of((row % per_col) * depth // LANES * LANES, LANES)

    def window_piece(way, step, at_core):
        at = basis_ring.origin(way, step, at_core)
        relation = at_core_index(at_core)
        source = basis_share.at[way % 2, sub_rows(way, at), pl.ds(first_lane, width)]
        target = window.at[way % 2, sub_rows(way, at), :]
        here = pltpu.make_async_copy(source, target, w_local.at[relation, way, step % 2])
        away = [
            pltpu.make_async_remote_copy(
                src_ref=source, dst_ref=target,
                send_sem=x_send.at[n, relation, way, step % 2],
                recv_sem=x_recv.at[relation, way, step],
                device_id=(row, other), device_id_type=MESH,
            )
            for n, other in enumerate(other_cols)
        ]
        return here, away

    def at_core_index(at_core):
        return 0 if at_core is core else 1

    other_core = 1 - core

    def start_window(step, at_core, chain):
        @pl.when(owner)
        def _():
            for way in (2 * chain, 2 * chain + 1):
                if step >= 2:
                    here, away = window_piece(way, step - 2, at_core)
                    here.wait()
                    for copy in away:
                        copy.wait_send()
                here, away = window_piece(way, step, at_core)
                for copy in away:
                    copy.start()
                here.start()

    def wait_handed(ring, step, chain=0):
        for way in (2 * chain, 2 * chain + 1):
            ring.handed(way, step).wait_recv()

    def basis_step(step, chain):
        basis_ring.advance(step, chain)
        if step == 0:
            if chain == 0:
                local[2].wait()
            start_window(0, core, chain)
        start_window(step + 1, core, chain)
        wait_handed(basis_ring, step, chain)
        start_window(step, other_core, chain)

    points = rows * own_points
    panel_len = points // 2
    screen = panel_len // 8
    tile = LANES
    out_copies = [
        pltpu.make_async_copy(mixed.at[s], mixed_out.at[s], local_sem.at[4 + s]) for s in range(spins)
    ]

    def mix():
        for s in range(spins):
            column = lax.broadcasted_iota(jnp.int32, (1, points), 1)
            column = jnp.where(column < panel_len, column + offsets[s, 0], column - panel_len + offsets[s, 1])
            column = column.astype(jnp.float32)

            @pl.loop(0, points // tile)
            def _(i):
                start = i * tile
                panel = start // panel_len
                line = lax.broadcasted_iota(jnp.int32, (tile, 1), 0) + (start - panel * panel_len) + offsets[s, panel]
                distance = jnp.abs(line.astype(jnp.float32) - column)
                at = pl.ds(pl.multiple_of(start, tile), tile)
                density = lax.dot_general(
                    orbitals[s, at, :], orbitals[s], (((1,), (1,)), ((), ())), preferred_element_type=jnp.float32
                )
                mixed[s, at, :] = (density * (screen / slots) / (screen + distance)).astype(jnp.bfloat16)

            out_copies[s].start()

    last = chips - 1
    done = 0
    early = max(last * 2 // 7, 1)
    for step in range(last):
        coefficient_ring.advance(step)
        if (step + 1) * early // last > done:
            basis_step(done, 0)
            basis_step(done, 1)
            done += 1
    for step in range(chips):
        wait_handed(coefficient_ring, step)
    local[0].wait()
    local[1].wait()

    total[...] = jnp.zeros_like(total)
    chunk = 9 * LANES if basis % (9 * LANES) == 0 else LANES

    @pl.loop(0, basis // chunk)
    def _(i):
        at = pl.ds(pl.multiple_of(i * chunk, chunk), chunk)
        total[...] += jnp.dot(own_colloc[:, at], all_coefficients[at, :], preferred_element_type=jnp.float32)

    slot = lax.broadcasted_iota(jnp.int32, total.shape, 1) + block * block_len
    own_orbitals[spin, :, block_lanes] = jnp.where(slot < occupied[spin], total[...], 0.0).astype(jnp.bfloat16)
    swaps = [
        pltpu.make_async_remote_copy(
            src_ref=own_orbitals.at[spin, :, block_lanes],
            dst_ref=own_orbitals.at[spin, :, block_lanes],
            send_sem=y_send.at[n], recv_sem=y_recv.at[n],
            device_id=(row, other), device_id_type=MESH,
        )
        for n, other in enumerate(other_cols)
    ]
    for copy in swaps:
        copy.start()
    for n in range(cols - 1):
        came = lax.rem(col + cols - 1 - n, cols)
        lanes = pl.ds(pl.multiple_of(came // spins * block_len, LANES), block_len)
        pltpu.make_async_remote_copy(
            src_ref=own_orbitals.at[spin, :, block_lanes],
            dst_ref=own_orbitals.at[came % spins, :, lanes],
            send_sem=y_send.at[n], recv_sem=y_recv.at[n],
            device_id=(row, came), device_id_type=MESH,
        ).wait_recv()
    orbital_ring.begin()
    own_out = pltpu.make_async_copy(own_orbitals, orbitals.at[:, point_rows(row), :], local_sem.at[3])
    own_out.start()
    left, sent = last - done, 0
    for n in range(left):
        if n == left - 1:
            while sent < last:
                orbital_ring.advance(sent)
                sent += 1
            for step in range(chips):
                wait_handed(orbital_ring, step)
            own_out.wait()
            mix()
        for chain in (0, 1):
            basis_step(done, chain)
            want = -(-(2 * n + chain + 1) * last // max(2 * left - 2, 1))
            while sent < min(want, last):
                orbital_ring.advance(sent)
                sent += 1
        done += 1
    for chain in (0, 1):
        wait_handed(basis_ring, last, chain)
        start_window(last, other_core, chain)
    for copy in out_copies:
        copy.wait()
    for copy in swaps:
        copy.wait_send()
    for ring in (coefficient_ring, basis_ring, orbital_ring):
        ring.finish_sends()

    @pl.when(owner)
    def _():
        for at_core in (core, other_core):
            for step in (last - 1, last):
                for way in range(4):
                    here, away = window_piece(way, step, at_core)
                    here.wait()
                    for copy in away:
                        copy.wait_send()

    @pl.when(jnp.logical_not(owner))
    def _():
        for at_core in (core, other_core):
            for step in range(chips):
                for way in range(4):
                    window_piece(way, step, at_core)[1][0].wait_recv()


def gathered(occupied, offsets, colloc, coefficients, rows, cols):
    spins, own_points, basis = colloc.shape
    depth, slots = coefficients.shape[1:]
    points, share, chips = own_points * rows, basis // cols, rows // 2
    slot_blocks = cols // spins
    block_len = slots // slot_blocks
    dma = pltpu.SemaphoreType.DMA
    ring = [dma((2, 2)), dma((2, chips - 1)), dma((2, 2)), dma((2, chips))]
    ring_of_two = [dma((4, 2)), dma((4, chips - 1)), dma((4, 2)), dma((4, chips))]
    hbm = pl.BlockSpec(memory_space=pltpu.HBM)
    smem = pl.BlockSpec(memory_space=pltpu.SMEM)
    return pl.pallas_call(
        functools.partial(transfers, rows, cols, slot_blocks),
        out_shape=(
            jax.ShapeDtypeStruct((spins, points, share), colloc.dtype),
            jax.ShapeDtypeStruct((spins, points, window_lanes(depth)), colloc.dtype),
            jax.ShapeDtypeStruct((spins, points, points), colloc.dtype),
        ),
        in_specs=[smem, smem, hbm, hbm],
        out_specs=(hbm,) * 3,
        scratch_shapes=[
            pltpu.VMEM((spins, points, slots), colloc.dtype),
            pltpu.VMEM((spins, points, points), colloc.dtype),
            pltpu.VMEM((basis, block_len), colloc.dtype),
            pltpu.VMEM((own_points, basis), colloc.dtype),
            pltpu.VMEM((spins, own_points, slots), colloc.dtype),
            pltpu.VMEM((own_points, block_len), jnp.float32),
            dma((4 + spins,)),
            *ring, *ring_of_two, *ring,
            dma((cols - 1, 2, 4, 2)), dma((2, 4, chips)), dma((2, 4, 2)),
            dma((cols - 1,)), dma((cols - 1,)),
        ],
        compiler_params=pltpu.CompilerParams(
            collective_id=0, has_side_effects=True, vmem_limit_bytes=60 * 2**20
        ),
    )(occupied, offsets, colloc, coefficients)


def product(depth, scale, window, mixed, basis_share, out, whole, weighted):
    @pl.when(pl.program_id(1) == 0)
    def _():
        whole[...] = lax.dot_general(
            window[0], mixed[0], (((0,), (1,)), ((), ())), preferred_element_type=jnp.float32
        )
        skip = pl.multiple_of(lax.axis_index("row") * depth % LANES, math.gcd(depth, LANES))
        weighted[...] = whole[pl.ds(skip, depth), :].astype(jnp.bfloat16)

    out[0] = (jnp.dot(weighted[...], basis_share[0], preferred_element_type=jnp.float32) * scale).astype(out.dtype)


def local(colloc, coefficients, occupied, offsets):
    rows = lax.axis_size("row")
    cols = lax.axis_size("col")
    depth = coefficients.shape[1]
    basis_share, window, mixed = gathered(occupied, offsets, colloc, coefficients, rows, cols)
    spins, points, share = basis_share.shape
    width = window.shape[2]
    tile = 9 * LANES if share % (9 * LANES) == 0 else LANES
    result = pl.pallas_call(
        functools.partial(product, depth, 1.0 / math.sqrt(points)),
        out_shape=jax.ShapeDtypeStruct((spins, depth, share), colloc.dtype),
        grid=(spins, share // tile),
        in_specs=[
            pl.BlockSpec((1, points, width), lambda s, m: (s, 0, 0)),
            pl.BlockSpec((1, points, points), lambda s, m: (s, 0, 0)),
            pl.BlockSpec((1, points, tile), lambda s, m: (s, 0, m)),
        ],
        out_specs=pl.BlockSpec((1, depth, tile), lambda s, m: (s, 0, m)),
        scratch_shapes=[pltpu.VMEM((width, points), jnp.float32), pltpu.VMEM((depth, points), colloc.dtype)],
        compiler_params=pltpu.CompilerParams(vmem_limit_bytes=60 * 2**20),
    )(window, mixed, basis_share)
    return jnp.transpose(result, (2, 0, 1))


def solution(mesh):
    placed = (P(None, "row", None), P(None, "row", None), P(), P())
    return jax.shard_map(
        local, mesh=mesh, in_specs=placed, out_specs=P("col", None, "row"), check_vma=False
    )
```

```python
import functools
import math

import jax
import jax.numpy as jnp
from jax import lax
from jax.experimental import pallas as pl
from jax.experimental.pallas import tpu as pltpu
from jax.sharding import PartitionSpec as P

MESH = pl.DeviceIdType.MESH
LANES = 128


def window_lanes(depth):
    over = LANES - math.gcd(depth, LANES)
    return -(-(depth + over) // LANES) * LANES


class Ring:
    def __init__(self, chains, place, own, piece, ring_send, ring_recv, pair_send, pair_recv):
        self.ways = range(2 * chains)
        self.place, self.own, self.piece = place, own, piece
        self.ring_send, self.ring_recv = ring_send, ring_recv
        self.pair_send, self.pair_recv = pair_send, pair_recv

    def origin(self, way, step, core):
        chips = self.place["chips"]
        back = -step if way % 2 == 0 else step
        return self.place["chip_at"](lax.rem(self.place["position"] + back + chips, chips)) * 2 + core

    def source(self, way, step):
        return self.own(way) if step == 0 else self.piece(way, self.origin(way, step, self.place["core"]))

    def hop(self, way, step):
        target = self.place["next"] if way % 2 == 0 else self.place["previous"]
        return pltpu.make_async_remote_copy(
            src_ref=self.source(way, step),
            dst_ref=self.piece(way, self.origin(way, step, self.place["core"])),
            send_sem=self.ring_send.at[way, step % 2],
            recv_sem=self.ring_recv.at[way, step],
            device_id=(target, self.place["col"]),
            device_id_type=MESH,
        )

    def landed(self, way, step):
        return pltpu.make_async_remote_copy(
            src_ref=self.source(way, step),
            dst_ref=self.piece(way, self.origin(way, step + 1, self.place["core"])),
            send_sem=self.ring_send.at[way, step % 2],
            recv_sem=self.ring_recv.at[way, step],
            device_id=(self.place["next"], self.place["col"]),
            device_id_type=MESH,
        )

    def hand(self, way, step):
        return pltpu.make_async_remote_copy(
            src_ref=self.source(way, step),
            dst_ref=self.piece(way, self.origin(way, step, self.place["core"])),
            send_sem=self.pair_send.at[way, step % 2],
            recv_sem=self.pair_recv.at[way, step],
            device_id=(self.place["sibling"], self.place["col"]),
            device_id_type=MESH,
        )

    def handed(self, way, step):
        return pltpu.make_async_remote_copy(
            src_ref=self.source(way, step),
            dst_ref=self.piece(way, self.origin(way, step, 1 - self.place["core"])),
            send_sem=self.pair_send.at[way, step % 2],
            recv_sem=self.pair_recv.at[way, step],
            device_id=(self.place["sibling"], self.place["col"]),
            device_id_type=MESH,
        )

    def begin(self):
        for way in self.ways:
            self.hop(way, 0).start()
        for way in self.ways:
            self.hand(way, 0).start()

    def advance(self, step, chain=0):
        chips = self.place["chips"]
        for way in (2 * chain, 2 * chain + 1):
            self.landed(way, step).wait_recv()
            if step + 1 < chips - 1:
                if step >= 1:
                    self.hop(way, step - 1).wait_send()
                self.hop(way, step + 1).start()
            if step >= 1:
                self.hand(way, step - 1).wait_send()
            self.hand(way, step + 1).start()

    def finish_sends(self):
        chips = self.place["chips"]
        for way in self.ways:
            for step in range(max(chips - 3, 0), chips - 1):
                self.hop(way, step).wait_send()
            for step in range(chips - 2, chips):
                self.hand(way, step).wait_send()


def transfers(
    rows, cols, slot_blocks, occupied, offsets, colloc, coefficients, basis_share, window, mixed_out,
    orbitals, mixed, all_coefficients, own_colloc, own_orbitals, total, local_sem,
    c_rs, c_rr, c_ps, c_pr, b_rs, b_rr, b_ps, b_pr, o_rs, o_rr, o_ps, o_pr,
    x_send, x_recv, w_local, y_send, y_recv,
):
    row, col = lax.axis_index("row"), lax.axis_index("col")
    spins, own_points, basis = colloc.shape
    depth, slots = coefficients.shape[1:]
    share = basis // cols
    width = window.shape[2]
    per_col = rows // cols
    chips = rows // 2
    side = chips // 2
    core, chip = row % 2, row // 2

    def chip_at(position):
        high = position // side
        return (position + high * (chips - 1 - 2 * position)) * 2 + high

    position = chip // 2 + (chip % 2) * (chips - 1 - 2 * (chip // 2))
    place = dict(
        chips=chips, chip_at=chip_at, position=position, core=core, col=col,
        next=chip_at(lax.rem(position + 1, chips)) * 2 + core,
        previous=chip_at(lax.rem(position + chips - 1, chips)) * 2 + core,
        sibling=chip * 2 + 1 - core,
    )
    other_cols = [lax.rem(col + shift, cols) for shift in range(1, cols)]
    spin, block = col % spins, col // spins
    block_len = slots // slot_blocks
    block_lanes = pl.ds(pl.multiple_of(block * block_len, LANES), block_len)
    share_start = pl.multiple_of(col * share, LANES)
    half = depth // 2

    barrier = pltpu.get_barrier_semaphore()
    for other in (place["next"], place["previous"], place["sibling"]):
        pl.semaphore_signal(barrier, inc=1, device_id=(other, col), device_id_type=MESH)
    for other in other_cols:
        pl.semaphore_signal(barrier, inc=1, device_id=(row, other), device_id_type=MESH)
    pl.semaphore_wait(barrier, 3 + len(other_cols))

    def point_rows(at):
        return pl.ds(pl.multiple_of(at * own_points, own_points), own_points)

    sub = own_points // 2

    def sub_rows(way, at):
        return pl.ds(pl.multiple_of(at * own_points + way // 2 * sub, sub), sub)

    coefficient_ring = Ring(
        1,
        place,
        lambda way: coefficients.at[spin, pl.ds(way * half, half), block_lanes],
        lambda way, at: all_coefficients.at[pl.ds(pl.multiple_of(at * depth + way * half, 16), half), :],
        c_rs, c_rr, c_ps, c_pr,
    )
    basis_ring = Ring(
        2,
        place,
        lambda way: colloc.at[way % 2, pl.ds(way // 2 * sub, sub), pl.ds(share_start, share)],
        lambda way, at: basis_share.at[way % 2, sub_rows(way, at), :],
        b_rs, b_rr, b_ps, b_pr,
    )
    orbital_ring = Ring(
        1,
        place,
        lambda way: own_orbitals.at[way],
        lambda way, at: orbitals.at[way, point_rows(at), :],
        o_rs, o_rr, o_ps, o_pr,
    )

    coefficient_ring.begin()
    basis_ring.begin()
    local = [
        pltpu.make_async_copy(
            coefficients.at[spin, :, block_lanes],
            all_coefficients.at[pl.ds(pl.multiple_of(row * depth, 16), depth), :],
            local_sem.at[0],
        ),
        pltpu.make_async_copy(colloc.at[spin], own_colloc, local_sem.at[1]),
        pltpu.make_async_copy(
            colloc.at[:, :, pl.ds(share_start, share)],
            basis_share.at[:, point_rows(row), :],
            local_sem.at[2],
        ),
    ]
    for copy in local:
        copy.start()

    owner = row // per_col == col
    first_lane = pl.multiple_of((row % per_col) * depth // LANES * LANES, LANES)

    def window_piece(way, step, at_core):
        at = basis_ring.origin(way, step, at_core)
        relation = at_core_index(at_core)
        source = basis_share.at[way % 2, sub_rows(way, at), pl.ds(first_lane, width)]
        target = window.at[way % 2, sub_rows(way, at), :]
        here = pltpu.make_async_copy(source, target, w_local.at[relation, way, step % 2])
        away = [
            pltpu.make_async_remote_copy(
                src_ref=source, dst_ref=target,
                send_sem=x_send.at[n, relation, way, step % 2],
                recv_sem=x_recv.at[relation, way, step],
                device_id=(row, other), device_id_type=MESH,
            )
            for n, other in enumerate(other_cols)
        ]
        return here, away

    def at_core_index(at_core):
        return 0 if at_core is core else 1

    other_core = 1 - core

    def start_window(step, at_core, chain):
        @pl.when(owner)
        def _():
            for way in (2 * chain, 2 * chain + 1):
                if step >= 2:
                    here, away = window_piece(way, step - 2, at_core)
                    here.wait()
                    for copy in away:
                        copy.wait_send()
                here, away = window_piece(way, step, at_core)
                for copy in away:
                    copy.start()
                here.start()

    def wait_handed(ring, step, chain=0):
        for way in (2 * chain, 2 * chain + 1):
            ring.handed(way, step).wait_recv()

    def basis_step(step, chain):
        basis_ring.advance(step, chain)
        if step == 0:
            if chain == 0:
                local[2].wait()
            start_window(0, core, chain)
        start_window(step + 1, core, chain)
        wait_handed(basis_ring, step, chain)
        start_window(step, other_core, chain)

    points = rows * own_points
    panel_len = points // 2
    screen = panel_len // 8
    tile = 2 * LANES
    out_copies = [
        pltpu.make_async_copy(mixed.at[s], mixed_out.at[s], local_sem.at[4 + s]) for s in range(spins)
    ]

    def mix(which):
        for s in which:
            column = lax.broadcasted_iota(jnp.int32, (1, points), 1)
            column = jnp.where(column < panel_len, column + offsets[s, 0], column - panel_len + offsets[s, 1])
            column = column.astype(jnp.float32)

            @pl.loop(0, points // tile)
            def _(i):
                start = i * tile
                panel = start // panel_len
                line = lax.broadcasted_iota(jnp.int32, (tile, 1), 0) + (start - panel * panel_len) + offsets[s, panel]
                distance = jnp.abs(line.astype(jnp.float32) - column)
                at = pl.ds(pl.multiple_of(start, tile), tile)
                density = lax.dot_general(
                    orbitals[s, at, :], orbitals[s], (((1,), (1,)), ((), ())), preferred_element_type=jnp.float32
                )
                mixed[s, at, :] = (density * (screen / slots) / (screen + distance)).astype(jnp.bfloat16)

            out_copies[s].start()

    last = chips - 1
    done = 0
    early = max(last * 2 // 7, 1)
    for step in range(last):
        coefficient_ring.advance(step)
        if (step + 1) * early // last > done:
            basis_step(done, 0)
            basis_step(done, 1)
            done += 1
    for step in range(chips):
        wait_handed(coefficient_ring, step)
    local[0].wait()
    local[1].wait()

    total[...] = jnp.zeros_like(total)
    chunk = 9 * LANES if basis % (9 * LANES) == 0 else LANES

    @pl.loop(0, basis // chunk)
    def _(i):
        at = pl.ds(pl.multiple_of(i * chunk, chunk), chunk)
        total[...] += jnp.dot(own_colloc[:, at], all_coefficients[at, :], preferred_element_type=jnp.float32)

    slot = lax.broadcasted_iota(jnp.int32, total.shape, 1) + block * block_len
    own_orbitals[spin, :, block_lanes] = jnp.where(slot < occupied[spin], total[...], 0.0).astype(jnp.bfloat16)
    swaps = [
        pltpu.make_async_remote_copy(
            src_ref=own_orbitals.at[spin, :, block_lanes],
            dst_ref=own_orbitals.at[spin, :, block_lanes],
            send_sem=y_send.at[n], recv_sem=y_recv.at[n],
            device_id=(row, other), device_id_type=MESH,
        )
        for n, other in enumerate(other_cols)
    ]
    for copy in swaps:
        copy.start()
    for n in range(cols - 1):
        came = lax.rem(col + cols - 1 - n, cols)
        lanes = pl.ds(pl.multiple_of(came // spins * block_len, LANES), block_len)
        pltpu.make_async_remote_copy(
            src_ref=own_orbitals.at[spin, :, block_lanes],
            dst_ref=own_orbitals.at[came % spins, :, lanes],
            send_sem=y_send.at[n], recv_sem=y_recv.at[n],
            device_id=(row, came), device_id_type=MESH,
        ).wait_recv()
    orbital_ring.begin()
    own_out = pltpu.make_async_copy(own_orbitals, orbitals.at[:, point_rows(row), :], local_sem.at[3])
    own_out.start()
    left, sent = last - done, 0
    mixed_spins = 0
    for n in range(left):
        if n >= left - 2:
            if mixed_spins == 0:
                while sent < last:
                    orbital_ring.advance(sent)
                    sent += 1
                for step in range(chips):
                    wait_handed(orbital_ring, step)
                own_out.wait()
            upto = spins if n == left - 1 else spins // 2
            mix(range(mixed_spins, upto))
            mixed_spins = upto
        for chain in (0, 1):
            basis_step(done, chain)
            want = -(-(2 * n + chain + 1) * last // max(2 * left - 4, 1))
            while sent < min(want, last):
                orbital_ring.advance(sent)
                sent += 1
        done += 1
    for chain in (0, 1):
        wait_handed(basis_ring, last, chain)
        start_window(last, other_core, chain)
    for copy in out_copies:
        copy.wait()
    for copy in swaps:
        copy.wait_send()
    for ring in (coefficient_ring, basis_ring, orbital_ring):
        ring.finish_sends()

    @pl.when(owner)
    def _():
        for at_core in (core, other_core):
            for step in (last - 1, last):
                for way in range(4):
                    here, away = window_piece(way, step, at_core)
                    here.wait()
                    for copy in away:
                        copy.wait_send()

    @pl.when(jnp.logical_not(owner))
    def _():
        for at_core in (core, other_core):
            for step in range(chips):
                for way in range(4):
                    window_piece(way, step, at_core)[1][0].wait_recv()


def gathered(occupied, offsets, colloc, coefficients, rows, cols):
    spins, own_points, basis = colloc.shape
    depth, slots = coefficients.shape[1:]
    points, share, chips = own_points * rows, basis // cols, rows // 2
    slot_blocks = cols // spins
    block_len = slots // slot_blocks
    dma = pltpu.SemaphoreType.DMA
    ring = [dma((2, 2)), dma((2, chips - 1)), dma((2, 2)), dma((2, chips))]
    ring_of_two = [dma((4, 2)), dma((4, chips - 1)), dma((4, 2)), dma((4, chips))]
    hbm = pl.BlockSpec(memory_space=pltpu.HBM)
    smem = pl.BlockSpec(memory_space=pltpu.SMEM)
    return pl.pallas_call(
        functools.partial(transfers, rows, cols, slot_blocks),
        out_shape=(
            jax.ShapeDtypeStruct((spins, points, share), colloc.dtype),
            jax.ShapeDtypeStruct((spins, points, window_lanes(depth)), colloc.dtype),
            jax.ShapeDtypeStruct((spins, points, points), colloc.dtype),
        ),
        in_specs=[smem, smem, hbm, hbm],
        out_specs=(hbm,) * 3,
        scratch_shapes=[
            pltpu.VMEM((spins, points, slots), colloc.dtype),
            pltpu.VMEM((spins, points, points), colloc.dtype),
            pltpu.VMEM((basis, block_len), colloc.dtype),
            pltpu.VMEM((own_points, basis), colloc.dtype),
            pltpu.VMEM((spins, own_points, slots), colloc.dtype),
            pltpu.VMEM((own_points, block_len), jnp.float32),
            dma((4 + spins,)),
            *ring, *ring_of_two, *ring,
            dma((cols - 1, 2, 4, 2)), dma((2, 4, chips)), dma((2, 4, 2)),
            dma((cols - 1,)), dma((cols - 1,)),
        ],
        compiler_params=pltpu.CompilerParams(
            collective_id=0, has_side_effects=True, vmem_limit_bytes=60 * 2**20
        ),
    )(occupied, offsets, colloc, coefficients)


def product(depth, scale, window, mixed, basis_share, out, whole, weighted):
    @pl.when(pl.program_id(1) == 0)
    def _():
        whole[...] = lax.dot_general(
            window[0], mixed[0], (((0,), (1,)), ((), ())), preferred_element_type=jnp.float32
        )
        skip = pl.multiple_of(lax.axis_index("row") * depth % LANES, math.gcd(depth, LANES))
        weighted[...] = whole[pl.ds(skip, depth), :].astype(jnp.bfloat16)

    out[0] = (jnp.dot(weighted[...], basis_share[0], preferred_element_type=jnp.float32) * scale).astype(out.dtype)


def local(colloc, coefficients, occupied, offsets):
    rows = lax.axis_size("row")
    cols = lax.axis_size("col")
    depth = coefficients.shape[1]
    basis_share, window, mixed = gathered(occupied, offsets, colloc, coefficients, rows, cols)
    spins, points, share = basis_share.shape
    width = window.shape[2]
    tile = next(n * LANES for n in (6, 3, 1) if share % (n * LANES) == 0)
    result = pl.pallas_call(
        functools.partial(product, depth, 1.0 / math.sqrt(points)),
        out_shape=jax.ShapeDtypeStruct((spins, depth, share), colloc.dtype),
        grid=(spins, share // tile),
        in_specs=[
            pl.BlockSpec((1, points, width), lambda s, m: (s, 0, 0)),
            pl.BlockSpec((1, points, points), lambda s, m: (s, 0, 0)),
            pl.BlockSpec((1, points, tile), lambda s, m: (s, 0, m)),
        ],
        out_specs=pl.BlockSpec((1, depth, tile), lambda s, m: (s, 0, m)),
        scratch_shapes=[pltpu.VMEM((width, points), jnp.float32), pltpu.VMEM((depth, points), colloc.dtype)],
        compiler_params=pltpu.CompilerParams(vmem_limit_bytes=60 * 2**20),
    )(window, mixed, basis_share)
    return jnp.transpose(result, (2, 0, 1))


def solution(mesh):
    placed = (P(None, "row", None), P(None, "row", None), P(), P())
    return jax.shard_map(
        local, mesh=mesh, in_specs=placed, out_specs=P("col", None, "row"), check_vma=False
    )
```
